32 devices in a mesh: groups: 2 (over x), rows: 16 (over z, y, core).
Axes of the slice: x: 2, y: 2, z: 4, core: 2. Of those that a mesh axis runs over, the one named last changes fastest.
Arguments:
- latent: bfloat16 [128, 256, 384], P(('groups', 'rows')), parts along dimension 0, may hold values from -6 to 6
- cache_frames: bfloat16 [2, 128, 256, 384], P(None, ('groups', 'rows')), parts along dimension 1, may hold values from -6 to 6
- norm_gain: float32 [384], replicated, may hold values from 0.1 to 1.9
- kernel: bfloat16 [3, 3, 3, 384, 384], replicated, may hold values from -0.0625 to 0.0625
- kernel_bias: float32 [384], replicated, may hold values from -3 to 3
Outputs:
- decoded: bfloat16 [128, 256, 384], P(('groups', 'rows')), parts along dimension 0
- next_cache: bfloat16 [128, 256, 384], P(('groups', 'rows')), parts along dimension 0
The draws below stay inside these ranges and needn't reach their ends.
There are 2 independent parts, one for each index of `groups`. The reference program is written for one: setup_inputs(seed, part) draws one part's arguments, and reference() takes and returns one part's arrays. A program takes and returns all parts, laid end to end along the dimension named above; an argument that names none is the same for every part. Nothing has to cross between parts.
All inputs are finite; a program needn't handle non-finite values.
Results may differ from the reference program's by a relative error of at most 0.0021.
Values may be sent and summed in bfloat16 or wider, within the bound.
A program may use at most 128 MiB of HBM per device.

```python
import jax
import jax.numpy as jnp
from jax import lax

CHANNELS = 384
GRID_COLS = 256
GRID_ROWS = 64


def block_scale(rng, shape, pieces, least, high):
    loudness = 1.0
    for position, shards_of in pieces:
        draws = jax.random.uniform(jax.random.fold_in(jax.random.fold_in(rng, 6), position), (shards_of,), jnp.float32, least / len(pieces), high / len(pieces))
        loudness = loudness * jnp.repeat(jnp.exp(draws), shape[position] // shards_of).reshape((-1,) + (1,) * (len(shape) - 1 - position))
    return loudness


def bell_draw(own_key, extent, deviation, limit, pieces=(), held_as=jnp.bfloat16):
    loudness = block_scale(own_key, extent, pieces, -0.22, 0.18) if pieces else 1.0
    values = jax.random.normal(own_key, extent, jnp.float32) * deviation * loudness
    return jnp.minimum(jnp.maximum(values, -limit), limit).astype(held_as)


def setup_inputs(seed: int = 0, part: int = 0) -> dict:
    seeds = jax.random.split(jax.random.key(seed), 6)
    part_keys = jax.random.split(jax.random.fold_in(seeds[5], part), 6)
    return {
        "latent": bell_draw(part_keys[0], (GRID_ROWS, GRID_COLS, CHANNELS), 1.0, 6.0, ((0, 16),)),
        "cache_frames": bell_draw(part_keys[1], (2, GRID_ROWS, GRID_COLS, CHANNELS), 1.0, 6.0, ((1, 16),)),
        "norm_gain": jnp.clip(1.0 + 0.18 * jax.random.normal(seeds[2], (CHANNELS,), jnp.float32), 0.1, 1.9),
        "kernel": bell_draw(seeds[3], (3, 3, 3, CHANNELS, CHANNELS), (27 * CHANNELS) ** -0.5, 0.0625),
        "kernel_bias": bell_draw(seeds[4], (CHANNELS,), 0.5, 3.0, (), jnp.float32),
    }


epsilon = 1e-06

def activate(values, gain):
    values = values.astype(jnp.float32)
    scaled = values * lax.rsqrt(lax.optimization_barrier(jnp.mean(values * values, axis=-1, keepdims=True)) + epsilon) * gain.astype(jnp.float32)
    return jax.nn.silu(scaled).astype(jnp.bfloat16)

def causal_conv(frames, weight, bias):
    out_rows = frames.shape[1] - 2
    out_cols = frames.shape[2] - 2
    channels = frames.shape[3]
    running = jnp.zeros((out_rows * out_cols, weight.shape[4]), jnp.float32)
    for tap_time in range(3):
        for tap_row in range(3):
            for tap_col in range(3):
                window = frames[tap_time, tap_row:tap_row + out_rows, tap_col:tap_col + out_cols, :]
                running = running + jnp.dot(window.reshape(out_rows * out_cols, channels), weight[tap_time, tap_row, tap_col], preferred_element_type=jnp.float32)
    return running.reshape(out_rows, out_cols, weight.shape[4]) + bias.astype(jnp.float32)

def reference(latent, cache_frames, norm_gain, kernel, kernel_bias):
    next_cache = activate(latent, norm_gain)
    frames = jnp.concatenate([cache_frames, next_cache[None]], axis=0)
    frames = jnp.pad(frames, ((0, 0), (1, 1), (1, 1), (0, 0)))
    branch = causal_conv(frames, kernel, kernel_bias)
    decoded = (latent.astype(jnp.float32) + branch).astype(jnp.bfloat16)
    return (decoded, next_cache)
```

```python
import functools

import jax
import jax.numpy as jnp
from jax import lax
from jax.experimental import pallas as pl
from jax.experimental.pallas import tpu as pltpu
from jax.sharding import PartitionSpec as P

epsilon = 1e-06
MESH = pl.DeviceIdType.MESH
f32 = jnp.float32
bf16 = jnp.bfloat16


def act(values, gain):
    values = values.astype(f32)
    scaled = values * lax.rsqrt(jnp.mean(values * values, axis=-1, keepdims=True) + epsilon) * gain
    return (scaled * jax.nn.sigmoid(scaled)).astype(bf16)


def kernel(
    shape, latent, cache, gain, weight, bias, decoded, next_cache,
    xs, ws, lat, acc, out, sent, got, x_sem, w_sem, o_sem, n_sem, send_sem, recv_sem,
):
    count, rows, cols, chan = shape
    last = rows - 1
    me = lax.axis_index("rows")
    has_up, has_down = me > 0, me < count - 1
    wide = 3 * chan

    def span(row):
        return pl.ds(row * cols, cols)

    def centre(time):
        return pl.ds(time * wide + chan, chan)

    x_in = {}
    for time in range(3):
        for row in range(rows):
            if time < 2:
                src, dst = cache.at[time, row], xs.at[span(row), centre(time)]
            else:
                src, dst = latent.at[row], lat.at[span(row)]
            x_in[time, row] = pltpu.make_async_copy(src, dst, x_sem.at[time, row])
    w_in = {}
    for time in range(3):
        for tap in range(3):
            for col in range(3):
                w_in[time, tap, col] = pltpu.make_async_copy(
                    weight.at[time, tap, col],
                    ws.at[pl.ds(time * wide + col * chan, chan), pl.ds(tap * chan, chan)],
                    w_sem.at[time, tap, col],
                )
    middle = list(range(1, last))
    for time in (0, 2, 1):
        for row in (0, last):
            x_in[time, row].start()
        if time == 0:
            for tap in (2, 0):
                for col in range(3):
                    w_in[time, tap, col].start()
    for time in (1, 2):
        for tap in (2, 0):
            for col in range(3):
                w_in[time, tap, col].start()
    for time in range(3):
        for row in middle:
            x_in[time, row].start()
    for time in range(3):
        for col in range(3):
            w_in[time, 1, col].start()

    barrier = pltpu.get_barrier_semaphore()

    @pl.when(has_up)
    def _():
        pl.semaphore_signal(barrier, inc=1, device_id={"rows": me - 1}, device_id_type=MESH)

    @pl.when(has_down)
    def _():
        pl.semaphore_signal(barrier, inc=1, device_id={"rows": me + 1}, device_id_type=MESH)

    place = lax.broadcasted_iota(jnp.int32, (cols, chan), 0)

    def shifts(time, row, value):
        value = value.astype(f32)
        before = jnp.where(place == 0, 0.0, pltpu.roll(value, 1, 0)).astype(bf16)
        after = jnp.where(place == cols - 1, 0.0, pltpu.roll(value, cols - 1, 0)).astype(bf16)
        xs[span(row), pl.ds(time * wide, chan)] = before
        xs[span(row), pl.ds(time * wide + 2 * chan, chan)] = after

    n_out = []

    def prepare(time, row):
        x_in[time, row].wait()
        if time < 2:
            shifts(time, row, xs[span(row), centre(time)])
        else:
            value = act(lat[span(row)], gain[...])
            xs[span(row), centre(time)] = value
            copy = pltpu.make_async_copy(
                xs.at[span(row), centre(time)], next_cache.at[row], n_sem.at[row]
            )
            copy.start()
            n_out.append(copy)
            shifts(time, row, value)

    def dot(row, times, taps):
        depth = pl.ds(times[0] * wide, len(times) * wide)
        width = pl.ds(taps[0] * chan, len(taps) * chan)
        return jnp.dot(xs[span(row), depth], ws[depth, width], preferred_element_type=f32)

    edges = ((0, 2), (last, 0))
    for time in range(3):
        for row, _ in edges:
            prepare(time, row)
        for row, tap in edges:
            for col in range(3):
                w_in[time, tap, col].wait()
    for side, (row, tap) in enumerate(edges):
        sent[side] = dot(row, (0, 1, 2), (tap,)).astype(bf16)

    pl.semaphore_wait(barrier, has_up.astype(jnp.int32) + has_down.astype(jnp.int32))

    def remote(side, target):
        return pltpu.make_async_remote_copy(
            src_ref=sent.at[side],
            dst_ref=got.at[side],
            send_sem=send_sem.at[side],
            recv_sem=recv_sem.at[side],
            device_id={"rows": target},
            device_id_type=MESH,
        )

    upward, downward = remote(0, me - 1), remote(1, me + 1)
    pl.when(has_up)(upward.start)
    pl.when(has_down)(downward.start)

    for row in middle:
        for time in range(3):
            prepare(time, row)
    for time in range(3):
        for col in range(3):
            w_in[time, 1, col].wait()

    started = set()

    def add(target, value):
        if target in started:
            acc[span(target)] += value
        else:
            started.add(target)
            acc[span(target)] = lat[span(target)].astype(f32) + bias[...] + value

    o_out = []

    def finish(target):
        out[span(target)] = acc[span(target)].astype(bf16)
        copy = pltpu.make_async_copy(out.at[span(target)], decoded.at[target], o_sem.at[target])
        copy.start()
        o_out.append(copy)

    left = {target: sum(0 <= target + tap - 1 < rows for tap in range(3)) for target in range(rows)}
    for row in middle + [0, last]:
        taps = [tap for tap in range(3) if 0 <= row - tap + 1 < rows]
        value = dot(row, (0, 1, 2), taps)
        for at, tap in enumerate(taps):
            target = row - tap + 1
            add(target, value[:, at * chan : (at + 1) * chan])
            left[target] -= 1
            if left[target] == 0 and 0 < target < last:
                finish(target)

    @pl.when(has_up)
    def _():
        upward.wait_send()
        downward.wait_recv()
        acc[span(0)] += got[1].astype(f32)

    finish(0)

    @pl.when(has_down)
    def _():
        downward.wait_send()
        upward.wait_recv()
        acc[span(last)] += got[0].astype(f32)

    finish(last)
    for copy in n_out + o_out:
        copy.wait()


def on_device(latent, cache_frames, norm_gain, weight, bias):
    rows, cols, chan = latent.shape
    count = lax.axis_size("rows")
    anywhere = pl.BlockSpec(memory_space=pl.ANY)
    vmem = pl.BlockSpec(memory_space=pltpu.VMEM)
    size = rows * cols
    DMA = pltpu.SemaphoreType.DMA
    return pl.pallas_call(
        functools.partial(kernel, (count, rows, cols, chan)),
        out_shape=[jax.ShapeDtypeStruct(latent.shape, bf16)] * 2,
        in_specs=[anywhere, anywhere, vmem, anywhere, vmem],
        out_specs=[anywhere, anywhere],
        scratch_shapes=[
            pltpu.VMEM((size, 9 * chan), bf16),
            pltpu.VMEM((9 * chan, 3 * chan), bf16),
            pltpu.VMEM((size, chan), bf16),
            pltpu.VMEM((size, chan), f32),
            pltpu.VMEM((size, chan), bf16),
            pltpu.VMEM((2, cols, chan), bf16),
            pltpu.VMEM((2, cols, chan), bf16),
            DMA((3, rows)),
            DMA((3, 3, 3)),
            DMA((rows,)),
            DMA((rows,)),
            DMA((2,)),
            DMA((2,)),
        ],
        compiler_params=pltpu.CompilerParams(
            collective_id=0, has_side_effects=True, vmem_limit_bytes=56 * 2**20
        ),
        cost_estimate=pl.CostEstimate(
            flops=2 * size * 27 * chan * chan,
            bytes_accessed=2 * (5 * size * chan + 27 * chan * chan),
            transcendentals=size * chan,
        ),
    )(latent, cache_frames, norm_gain.reshape(1, chan), weight, bias.reshape(1, chan))


def solution(mesh):
    in_specs = (
        P(("groups", "rows"), None, None),
        P(None, ("groups", "rows"), None, None),
        P(),
        P(),
        P(),
    )
    out_specs = (P(("groups", "rows"), None, None), P(("groups", "rows"), None, None))
    return jax.shard_map(
        on_device, mesh=mesh, in_specs=in_specs, out_specs=out_specs, check_vma=False
    )
```

```python
import functools

import jax
import jax.numpy as jnp
from jax import lax
from jax.experimental import pallas as pl
from jax.experimental.pallas import tpu as pltpu
from jax.sharding import PartitionSpec as P

epsilon = 1e-06
MESH = pl.DeviceIdType.MESH
f32 = jnp.float32
bf16 = jnp.bfloat16


def act(values, gain):
    values = values.astype(f32)
    scaled = values * lax.rsqrt(jnp.mean(values * values, axis=-1, keepdims=True) + epsilon) * gain
    return (scaled * jax.nn.sigmoid(scaled)).astype(bf16)


def kernel(
    shape, latent, cache, gain_in, weight, bias_in, acc, fresh, got,
    xs, ws, lat, part, sent, gain, bias, p_sem, x_sem, w_sem, send_sem, recv_sem,
):
    count, rows, cols, chan = shape
    last = rows - 1
    me = lax.axis_index("rows")
    has_up, has_down = me > 0, me < count - 1
    wide = 3 * chan

    def span(row, many=1):
        return pl.ds(row * cols, many * cols)

    def centre(time):
        return pl.ds(time * wide + chan, chan)

    x_in = {}
    for time in range(3):
        for row in range(rows):
            if time < 2:
                src, dst = cache.at[time, row], xs.at[span(row), centre(time)]
            else:
                src, dst = latent.at[row], lat.at[span(row)]
            x_in[time, row] = pltpu.make_async_copy(src, dst, x_sem.at[time, row])
    w_in = {}
    for time in range(3):
        for tap in range(3):
            for col in range(3):
                w_in[time, tap, col] = pltpu.make_async_copy(
                    weight.at[time, tap, col],
                    ws.at[pl.ds(time * wide + col * chan, chan), pl.ds(tap * chan, chan)],
                    w_sem.at[time, tap, col],
                )

    def weights(time, taps, act):
        for tap in taps:
            for col in range(3):
                getattr(w_in[time, tap, col], act)()

    vectors = [
        pltpu.make_async_copy(src, dst, p_sem.at[at])
        for at, (src, dst) in enumerate(((gain_in, gain), (bias_in, bias)))
    ]
    middle = list(range(1, last))
    for copy in vectors:
        copy.start()
    for time in (2, 0, 1):
        for row in (0, last):
            x_in[time, row].start()
    weights(0, (2, 0), "start")
    for row in middle:
        for time in range(3):
            x_in[time, row].start()
    weights(1, (2, 0), "start")
    weights(2, (2, 0), "start")
    for time in range(3):
        weights(time, (1,), "start")

    barrier = pltpu.get_barrier_semaphore()

    @pl.when(has_up)
    def _():
        pl.semaphore_signal(barrier, inc=1, device_id={"rows": me - 1}, device_id_type=MESH)

    @pl.when(has_down)
    def _():
        pl.semaphore_signal(barrier, inc=1, device_id={"rows": me + 1}, device_id_type=MESH)

    place = lax.broadcasted_iota(jnp.int32, (cols, chan), 0)

    def shifts(time, row, value):
        value = value.astype(f32)
        before = jnp.where(place == 0, 0.0, pltpu.roll(value, 1, 0)).astype(bf16)
        after = jnp.where(place == cols - 1, 0.0, pltpu.roll(value, cols - 1, 0)).astype(bf16)
        xs[span(row), pl.ds(time * wide, chan)] = before
        xs[span(row), pl.ds(time * wide + 2 * chan, chan)] = after

    def prepare(row):
        value = act(lat[span(row)], gain[...].reshape(1, chan))
        xs[span(row), centre(2)] = value
        fresh[row] = value
        shifts(2, row, value)
        for time in range(2):
            shifts(time, row, xs[span(row), centre(time)])

    def dot(rows_of, times, taps):
        depth = pl.ds(times[0] * wide, len(times) * wide)
        width = pl.ds(taps[0] * chan, len(taps) * chan)
        return jnp.dot(xs[rows_of, depth], ws[depth, width], preferred_element_type=f32)

    edges = ((0, 2), (last, 0))
    for copy in vectors:
        copy.wait()
    for row, _ in edges:
        for time in range(3):
            x_in[time, row].wait()
        prepare(row)
    for row in middle:
        for time in range(3):
            x_in[time, row].wait()
    todo = list(middle)
    for time in range(3):
        weights(time, (2, 0), "wait")
        for side, (row, tap) in enumerate(edges):
            value = dot(span(row), (time,), (tap,))
            if time == 0:
                part[side] = value
            elif time == 1:
                part[side] += value
            else:
                sent[side] = (part[side] + value).astype(bf16)
        if time < 2:
            share = -(-len(middle) // 2)
            for row in todo[:share]:
                prepare(row)
            todo = todo[share:]

    pl.semaphore_wait(barrier, has_up.astype(jnp.int32) + has_down.astype(jnp.int32))

    def remote(side, target):
        return pltpu.make_async_remote_copy(
            src_ref=sent.at[side],
            dst_ref=got.at[side],
            send_sem=send_sem.at[side],
            recv_sem=recv_sem.at[side],
            device_id={"rows": target},
            device_id_type=MESH,
        )

    upward, downward = remote(0, me - 1), remote(1, me + 1)
    pl.when(has_up)(upward.start)
    pl.when(has_down)(downward.start)
    for time in range(3):
        weights(time, (1,), "wait")

    started = set()

    def add(target, value):
        if target in started:
            acc[target] += value
        else:
            started.add(target)
            acc[target] = lat[span(target)].astype(f32) + bias[...].reshape(1, chan) + value

    def own(row, many, taps):
        value = dot(span(row, many), (0, 1, 2), taps)
        for step in range(many):
            for at, tap in enumerate(taps):
                add(
                    row + step - tap + 1,
                    value[step * cols : (step + 1) * cols, at * chan : (at + 1) * chan],
                )

    for row in middle[::2]:
        own(row, min(2, last - row), (0, 1, 2))
    own(0, 1, (0, 1))
    own(last, 1, (1, 2))

    @pl.when(has_up)
    def _():
        upward.wait_send()
        downward.wait_recv()

    @pl.when(has_down)
    def _():
        downward.wait_send()
        upward.wait_recv()

    @pl.when(jnp.logical_not(has_up))
    def _():
        got[1] = jnp.zeros((cols, chan), bf16)

    @pl.when(jnp.logical_not(has_down))
    def _():
        got[0] = jnp.zeros((cols, chan), bf16)


def writer(acc, fresh, got, decoded, next_cache, out, sem):
    rows = acc.shape[0]
    copies = [pltpu.make_async_copy(fresh, next_cache, sem.at[rows])]
    copies[0].start()
    for row in range(rows):
        value = acc[row]
        if row == 0:
            value = value + got[1].astype(f32)
        if row == rows - 1:
            value = value + got[0].astype(f32)
        out[row] = value.astype(bf16)
        copy = pltpu.make_async_copy(out.at[row], decoded.at[row], sem.at[row])
        copy.start()
        copies.append(copy)
    for copy in copies:
        copy.wait()


def on_device(latent, cache_frames, norm_gain, weight, bias):
    rows, cols, chan = latent.shape
    count = lax.axis_size("rows")
    arguments = (latent, cache_frames, norm_gain, weight, bias)
    hbm = pl.BlockSpec(memory_space=pltpu.HBM)
    vmem = pl.BlockSpec(memory_space=pltpu.VMEM)
    size = rows * cols
    DMA = pltpu.SemaphoreType.DMA
    acc, fresh, got = pl.pallas_call(
        functools.partial(kernel, (count, rows, cols, chan)),
        out_shape=[
            pltpu.VMEM((rows, cols, chan), f32),
            pltpu.VMEM((rows, cols, chan), bf16),
            pltpu.VMEM((2, cols, chan), bf16),
        ],
        in_specs=[hbm] * 5,
        out_specs=[vmem] * 3,
        scratch_shapes=[
            pltpu.VMEM((size, 9 * chan), bf16),
            pltpu.VMEM((9 * chan, 3 * chan), bf16),
            pltpu.VMEM((size, chan), bf16),
            pltpu.VMEM((2, cols, chan), f32),
            pltpu.VMEM((2, cols, chan), bf16),
            pltpu.VMEM((chan,), f32),
            pltpu.VMEM((chan,), f32),
            DMA((2,)),
            DMA((3, rows)),
            DMA((3, 3, 3)),
            DMA((2,)),
            DMA((2,)),
        ],
        compiler_params=pltpu.CompilerParams(
            collective_id=0, has_side_effects=True, vmem_limit_bytes=40 * 2**20
        ),
        cost_estimate=pl.CostEstimate(
            flops=2 * size * 27 * chan * chan,
            bytes_accessed=2 * (5 * size * chan + 27 * chan * chan),
            transcendentals=size * chan,
        ),
    )(*(pltpu.with_memory_space_constraint(array, pltpu.HBM) for array in arguments))
    return pl.pallas_call(
        writer,
        out_shape=[jax.ShapeDtypeStruct(latent.shape, bf16)] * 2,
        in_specs=[vmem] * 3,
        out_specs=[hbm] * 2,
        scratch_shapes=[pltpu.VMEM((rows, cols, chan), bf16), DMA((rows + 1,))],
        compiler_params=pltpu.CompilerParams(vmem_limit_bytes=16 * 2**20),
        cost_estimate=pl.CostEstimate(
            flops=size * chan, bytes_accessed=10 * size * chan, transcendentals=0
        ),
    )(acc, fresh, got)


def solution(mesh):
    in_specs = (
        P(("groups", "rows"), None, None),
        P(None, ("groups", "rows"), None, None),
        P(),
        P(),
        P(),
    )
    out_specs = (P(("groups", "rows"), None, None), P(("groups", "rows"), None, None))
    return jax.shard_map(
        on_device, mesh=mesh, in_specs=in_specs, out_specs=out_specs, check_vma=False
    )
```

```python
import functools

import jax
import jax.numpy as jnp
from jax import lax
from jax.experimental import pallas as pl
from jax.experimental.pallas import tpu as pltpu
from jax.sharding import PartitionSpec as P

epsilon = 1e-06
MESH = pl.DeviceIdType.MESH
f32 = jnp.float32
bf16 = jnp.bfloat16


def act(values, gain):
    values = values.astype(f32)
    scaled = values * lax.rsqrt(jnp.mean(values * values, axis=-1, keepdims=True) + epsilon) * gain
    return (scaled * jax.nn.sigmoid(scaled)).astype(bf16)


def kernel(
    shape, latent, cache, gain_in, weight, bias_in, acc, fresh, got,
    xs, ws, lat, part, sent, gain, bias, p_sem, x_sem, w_sem, send_sem, recv_sem,
):
    count, rows, cols, chan = shape
    last = rows - 1
    me = lax.axis_index("rows")
    has_up, has_down = me > 0, me < count - 1
    wide = 3 * chan

    def span(row, many=1):
        return pl.ds(row * cols, many * cols)

    def centre(time):
        return pl.ds(time * wide + chan, chan)

    x_in = {}
    for time in range(3):
        for row in range(rows):
            if time < 2:
                src, dst = cache.at[time, row], xs.at[span(row), centre(time)]
            else:
                src, dst = latent.at[row], lat.at[span(row)]
            x_in[time, row] = pltpu.make_async_copy(src, dst, x_sem.at[time, row])
    w_in = {}
    for time in range(3):
        for tap in range(3):
            for col in range(3):
                w_in[time, tap, col] = pltpu.make_async_copy(
                    weight.at[time, tap, col],
                    ws.at[pl.ds(time * wide + col * chan, chan), pl.ds(tap * chan, chan)],
                    w_sem.at[time, tap, col],
                )

    def weights(time, taps, act):
        for tap in taps:
            for col in range(3):
                getattr(w_in[time, tap, col], act)()

    vectors = [
        pltpu.make_async_copy(src, dst, p_sem.at[at])
        for at, (src, dst) in enumerate(((gain_in, gain), (bias_in, bias)))
    ]
    middle = list(range(1, last))
    for copy in vectors:
        copy.start()
    for time in range(3):
        for row in (0, last):
            x_in[time, row].start()
        weights(time, (2, 0), "start")
    for row in middle:
        for time in range(3):
            x_in[time, row].start()
    for time in range(3):
        weights(time, (1,), "start")

    barrier = pltpu.get_barrier_semaphore()

    @pl.when(has_up)
    def _():
        pl.semaphore_signal(barrier, inc=1, device_id={"rows": me - 1}, device_id_type=MESH)

    @pl.when(has_down)
    def _():
        pl.semaphore_signal(barrier, inc=1, device_id={"rows": me + 1}, device_id_type=MESH)

    place = lax.broadcasted_iota(jnp.int32, (16, chan), 0)

    def shifts(time, row, value):
        value = value.astype(f32)
        before = pltpu.roll(value, 1, 0)
        after = pltpu.roll(value, cols - 1, 0)
        head = jnp.where(place == 0, 0.0, before[:16])
        tail = jnp.where(place == 15, 0.0, after[cols - 16 :])
        before = jnp.concatenate([head, before[16:]], axis=0).astype(bf16)
        after = jnp.concatenate([after[: cols - 16], tail], axis=0).astype(bf16)
        xs[span(row), pl.ds(time * wide, chan)] = before
        xs[span(row), pl.ds(time * wide + 2 * chan, chan)] = after

    def prepare(time, row):
        if time < 2:
            shifts(time, row, xs[span(row), centre(time)])
            return
        value = act(lat[span(row)], gain[...].reshape(1, chan))
        xs[span(row), centre(2)] = value
        fresh[row] = value
        shifts(2, row, value)

    def dot(rows_of, times, taps):
        depth = pl.ds(times[0] * wide, len(times) * wide)
        width = pl.ds(taps[0] * chan, len(taps) * chan)
        return jnp.dot(xs[rows_of, depth], ws[depth, width], preferred_element_type=f32)

    edges = ((0, 2), (last, 0))
    for copy in vectors:
        copy.wait()
    for row, _ in edges:
        x_in[0, row].wait()
    for row, _ in edges:
        prepare(0, row)
    for time in range(3):
        weights(time, (2, 0), "wait")
        if time < 2:
            for row, _ in edges:
                x_in[time + 1, row].wait()
        for side, (row, tap) in enumerate(edges):
            value = dot(span(row), (time,), (tap,))
            if time == 0:
                part[side] = value
            elif time == 1:
                part[side] += value
            else:
                sent[side] = (part[side] + value).astype(bf16)
            if time < 2:
                prepare(time + 1, row)

    pl.semaphore_wait(barrier, has_up.astype(jnp.int32) + has_down.astype(jnp.int32))

    def remote(side, target):
        return pltpu.make_async_remote_copy(
            src_ref=sent.at[side],
            dst_ref=got.at[side],
            send_sem=send_sem.at[side],
            recv_sem=recv_sem.at[side],
            device_id={"rows": target},
            device_id_type=MESH,
        )

    upward, downward = remote(0, me - 1), remote(1, me + 1)
    pl.when(has_up)(upward.start)
    pl.when(has_down)(downward.start)
    for row in middle:
        for time in range(3):
            x_in[time, row].wait()
    for time in range(3):
        weights(time, (1,), "wait")

    started = set()

    def add(target, value):
        if target in started:
            acc[target] += value
        else:
            started.add(target)
            acc[target] = lat[span(target)].astype(f32) + bias[...].reshape(1, chan) + value

    def own(row, many, taps):
        value = dot(span(row, many), (0, 1, 2), taps)
        for step in range(many):
            for at, tap in enumerate(taps):
                add(
                    row + step - tap + 1,
                    value[step * cols : (step + 1) * cols, at * chan : (at + 1) * chan],
                )

    own(0, 1, (0, 1))
    for row in middle:
        for time in range(3):
            prepare(time, row)
    own(last, 1, (1, 2))
    for row in middle[::2]:
        own(row, min(2, last - row), (0, 1, 2))

    @pl.when(has_up)
    def _():
        upward.wait_send()
        downward.wait_recv()

    @pl.when(has_down)
    def _():
        downward.wait_send()
        upward.wait_recv()

    @pl.when(jnp.logical_not(has_up))
    def _():
        got[1] = jnp.zeros((cols, chan), bf16)

    @pl.when(jnp.logical_not(has_down))
    def _():
        got[0] = jnp.zeros((cols, chan), bf16)


def writer(acc, fresh, got, decoded, next_cache, out, sem):
    rows = acc.shape[0]
    copies = [pltpu.make_async_copy(fresh, next_cache, sem.at[rows])]
    copies[0].start()
    for row in range(rows):
        value = acc[row]
        if row == 0:
            value = value + got[1].astype(f32)
        if row == rows - 1:
            value = value + got[0].astype(f32)
        out[row] = value.astype(bf16)
        copy = pltpu.make_async_copy(out.at[row], decoded.at[row], sem.at[row])
        copy.start()
        copies.append(copy)
    for copy in copies:
        copy.wait()


def on_device(latent, cache_frames, norm_gain, weight, bias):
    rows, cols, chan = latent.shape
    count = lax.axis_size("rows")
    arguments = (latent, cache_frames, norm_gain, weight, bias)
    hbm = pl.BlockSpec(memory_space=pltpu.HBM)
    vmem = pl.BlockSpec(memory_space=pltpu.VMEM)
    size = rows * cols
    DMA = pltpu.SemaphoreType.DMA
    acc, fresh, got = pl.pallas_call(
        functools.partial(kernel, (count, rows, cols, chan)),
        out_shape=[
            pltpu.VMEM((rows, cols, chan), f32),
            pltpu.VMEM((rows, cols, chan), bf16),
            pltpu.VMEM((2, cols, chan), bf16),
        ],
        in_specs=[hbm] * 5,
        out_specs=[vmem] * 3,
        scratch_shapes=[
            pltpu.VMEM((size, 9 * chan), bf16),
            pltpu.VMEM((9 * chan, 3 * chan), bf16),
            pltpu.VMEM((size, chan), bf16),
            pltpu.VMEM((2, cols, chan), f32),
            pltpu.VMEM((2, cols, chan), bf16),
            pltpu.VMEM((chan,), f32),
            pltpu.VMEM((chan,), f32),
            DMA((2,)),
            DMA((3, rows)),
            DMA((3, 3, 3)),
            DMA((2,)),
            DMA((2,)),
        ],
        compiler_params=pltpu.CompilerParams(
            collective_id=0, has_side_effects=True, vmem_limit_bytes=40 * 2**20
        ),
        cost_estimate=pl.CostEstimate(
            flops=2 * size * 27 * chan * chan,
            bytes_accessed=2 * (5 * size * chan + 27 * chan * chan),
            transcendentals=size * chan,
        ),
    )(*(pltpu.with_memory_space_constraint(array, pltpu.HBM) for array in arguments))
    return pl.pallas_call(
        writer,
        out_shape=[jax.ShapeDtypeStruct(latent.shape, bf16)] * 2,
        in_specs=[vmem] * 3,
        out_specs=[hbm] * 2,
        scratch_shapes=[pltpu.VMEM((rows, cols, chan), bf16), DMA((rows + 1,))],
        compiler_params=pltpu.CompilerParams(vmem_limit_bytes=16 * 2**20),
        cost_estimate=pl.CostEstimate(
            flops=size * chan, bytes_accessed=10 * size * chan, transcendentals=0
        ),
    )(acc, fresh, got)


def solution(mesh):
    in_specs = (
        P(("groups", "rows"), None, None),
        P(None, ("groups", "rows"), None, None),
        P(),
        P(),
        P(),
    )
    out_specs = (P(("groups", "rows"), None, None), P(("groups", "rows"), None, None))
    return jax.shard_map(
        on_device, mesh=mesh, in_specs=in_specs, out_specs=out_specs, check_vma=False
    )
```
